1024 devices in a mesh: enc: 16 (over z, core), roll: 64 (over x, y).
Axes of the slice: x: 8, y: 8, z: 8, core: 2. Of those that a mesh axis runs over, the one named last changes fastest.
Arguments:
- row_grads: bfloat16 [16, 2048, 8192], P('enc', 'roll'), may hold values from -1.5 to 1.5
- row_dest: int32 [16, 2048], P('enc', 'roll'), may hold values from 0 to 128, as said below
- merger_in: bfloat16 [16, 128, 5120], P('enc'), may hold values from -6 to 6
- hidden_pre: bfloat16 [16, 128, 5120], P('enc'), may hold values from -8 to 8
- w_second: bfloat16 [5120, 8192], P(None, 'roll'), may hold values from -0.25 to 0.25
Outputs:
- pre_grads: bfloat16 [16, 128, 5120], P('enc', None, 'roll')
- grad_first: float32 [5120, 5120], P('enc', 'roll')
- grad_second: float32 [5120, 8192], P('enc', 'roll')
The draws below stay inside these ranges and needn't reach their ends.
Inputs may be any that keep to these rules, and one draw needn't show every extreme that they name: `row_dest`: slot j of rollout device r in a group (slots r * 32 to (r + 1) * 32 - 1) holds 128 for an unused slot or a merged row of its prompt, in [(r // 16) * 32, (r // 16 + 1) * 32); the used rows of one device are distinct.
All inputs are finite; a program needn't handle non-finite values.
Results may differ from the reference program's by a relative error of at most 0.017.
Values may be sent and summed in bfloat16 or wider, within the bound.
A program may use at most 32 MiB of HBM per device.

```python
import math
import jax
import jax.numpy as jnp
from jax import lax

D = 8192
MW = 5120
ROWS_DEV = 32
GROUPS = 16
SHARDS = 64
ROLLOUTS = 16
MERGED = 128
ROLL_ROWS = 2048
ALLROWS = 2048


def draw_row_dest(key, part):
    key_order = jax.random.fold_in(key, 11)
    key_live = jax.random.fold_in(key, 23)
    scores = jax.random.randint(key_order, (GROUPS, SHARDS, ROWS_DEV), 0, 1048576)
    within = jnp.arange(ROWS_DEV, dtype=jnp.int32)
    order = jnp.argsort(scores * ROWS_DEV + within[None, None, :], axis=-1).astype(jnp.int32)
    live = jax.random.randint(key_live, (GROUPS, SHARDS), ROWS_DEV // 2, ROWS_DEV + 1)
    shard_ids = jnp.arange(SHARDS, dtype=jnp.int32)
    rollout = shard_ids % ROLLOUTS
    live = jnp.where(rollout[None, :] == 0, ROWS_DEV, jnp.where(rollout[None, :] == ROLLOUTS - 1, ROWS_DEV // 2, live))
    base = shard_ids // ROLLOUTS * ROWS_DEV
    target = base[None, :, None] + order
    dest = jnp.where(within[None, None, :] < live[:, :, None], target, MERGED)
    return dest.reshape(GROUPS, ROLL_ROWS).astype(jnp.int32)


def raised(array, own_key, source, target, parts, factor):
    def block_of(dim):
        return (jnp.arange(array.shape[dim]) // (array.shape[dim] // parts)).reshape((-1,) + (1,) * (array.ndim - 1 - dim))

    first = jax.random.permutation(own_key, parts)[block_of(target)]
    far = (block_of(target) + parts // 2) % parts
    return jnp.where((block_of(source) == first) | (block_of(source) == far), factor * array, array)


def shard_levels(stream_key, extent, shards, least, high):
    def one(axis_at, blocks):
        steps = jax.random.uniform(jax.random.fold_in(jax.random.fold_in(stream_key, 6), axis_at), (blocks,), jnp.float32, least / len(shards), high / len(shards))
        return jnp.repeat(jnp.exp(steps), extent[axis_at] // blocks).reshape((-1,) + (1,) * (len(extent) - axis_at - 1))

    gain = one(*shards[0])
    for cut in shards[1:]:
        gain = gain * one(*cut)
    return gain


def centred(stream_key, dims, spread, limit, shards=(), kind=jnp.bfloat16):
    drawn = spread * jax.random.normal(stream_key, dims, jnp.float32)
    if shards:
        drawn = drawn * shard_levels(stream_key, dims, shards, -0.22, 0.18)
    return jnp.clip(drawn, -limit, limit).astype(kind)


def heavy_noise(rng, dims, deviation, reach, split, heavy, held_as=jnp.bfloat16):
    array = deviation * jax.random.normal(rng, dims, jnp.float32)
    if split:
        array = array * shard_levels(rng, dims, split, -0.22, 0.18)
    return jnp.clip(raised(array, jax.random.fold_in(rng, 3), *heavy), -reach, reach).astype(held_as)


def setup_inputs(seed: int = 0) -> dict:
    seeds = jax.random.split(jax.random.key(seed), 6)
    row_grads = centred(seeds[0], (GROUPS, ROLL_ROWS, D), 0.25, 1.5, ((0, 16), (1, 64)))
    row_dest = draw_row_dest(jax.random.fold_in(seeds[5], 71), 0)
    merger_in = centred(seeds[2], (GROUPS, MERGED, MW), 1.0, 6.0, ((0, 16),))
    hidden_pre = centred(seeds[3], (GROUPS, MERGED, MW), 1.5, 8.0, ((0, 16),))
    w_second = heavy_noise(seeds[4], (MW, D), MW ** -0.5, 0.25, ((1, 64),), (1, 0, 64, 4.0))
    return {"row_grads": row_grads, "row_dest": row_dest, "merger_in": merger_in, "hidden_pre": hidden_pre, "w_second": w_second}


inv_root_two = 1.0 / math.sqrt(2.0)
inv_root_two_pi = 1.0 / math.sqrt(2.0 * math.pi)

def gelu_slope(values):
    return 0.5 * (1.0 + lax.erf(values * inv_root_two)) + values * jnp.exp(-0.5 * values * values) * inv_root_two_pi

def to_bfloat(values):
    return lax.optimization_barrier(values.astype(jnp.bfloat16)).astype(jnp.float32)

def reference(row_grads, row_dest, merger_in, hidden_pre, w_second):
    factor = 1.0 / math.sqrt(ALLROWS)
    grad_first = jnp.zeros((MW, MW), jnp.float32)
    grad_second = jnp.zeros((MW, D), jnp.float32)
    results = []
    for group in range(GROUPS):
        sums = jax.ops.segment_sum(row_grads[group].astype(jnp.float32), row_dest[group].astype(jnp.int32), num_segments=MERGED + 1)[:MERGED]
        merged = sums.astype(jnp.bfloat16)
        before = hidden_pre[group].astype(jnp.float32)
        hidden = jax.nn.gelu(before, approximate=False).astype(jnp.bfloat16)
        units = jnp.dot(merged, w_second.T, preferred_element_type=jnp.float32)
        grads = (units * gelu_slope(before)).astype(jnp.bfloat16)
        results.append(grads)
        term_second = jnp.dot(hidden.T, merged, preferred_element_type=jnp.float32) * factor
        term_first = jnp.dot(merger_in[group].T, grads, preferred_element_type=jnp.float32) * factor
        grad_second = grad_second + to_bfloat(term_second)
        grad_first = grad_first + to_bfloat(term_first)
    return (jnp.stack(results), grad_first, grad_second)
```

```python
import functools
import math

import jax
import jax.numpy as jnp
from jax import lax
from jax.experimental import pallas as pl
from jax.experimental.pallas import tpu as pltpu
from jax.sharding import PartitionSpec as P

MESH = pl.DeviceIdType.MESH
inv_root_two = 1.0 / math.sqrt(2.0)
inv_root_two_pi = 1.0 / math.sqrt(2.0 * math.pi)
N = 8
SLOTS = 32
LANES = 128
MERGED = 128
UNITS = 80
OWN = 320
PAIR = 640
PADDED = 384
PROMPT_X = 2


def gelu(v):
    return v * (0.5 * (1.0 + lax.erf(v * inv_root_two)))


def gelu_slope(v):
    return 0.5 * (1.0 + lax.erf(v * inv_root_two)) + v * jnp.exp(-0.5 * v * v) * inv_root_two_pi


def kernel(
    factor,
    rows_hbm, dest_ref, merger_hbm, before_hbm, w_hbm,
    pre_ref, first_ref, second_ref,
    rows, merger, before, slot_send, slot_recv, part_send, part_recv, gathered, other_merged,
    weights, hidden, other_hidden, inputs, other_inputs, term_send, term_recv,
    unit_send, unit_recv, other_pre, own_pre, last_send, last_recv,
    local_sem, slot_s, slot_r, part_s, part_r, gather_s, gather_r, wy_s, wy_r, wz_s, wz_r, wc_s, wc_r,
    unit_s, unit_r, term_s, term_r, last_s, last_r, core_s, core_r,
):
    enc = lax.axis_index("enc")
    roll = lax.axis_index("roll")
    z, core = enc // 2, enc % 2
    x, y = roll // N, roll % N

    def at_y(other):
        return (enc, x * N + other)

    def at_x(other):
        return (enc, other * N + y)

    def at_z(other):
        return (other * 2 + core, roll)

    twin = (z * 2 + (1 - core), roll)

    def remote(src, dst, send, recv, device):
        return pltpu.make_async_remote_copy(
            src_ref=src, dst_ref=dst, send_sem=send, recv_sem=recv, device_id=device, device_id_type=MESH
        )

    barrier = pltpu.get_barrier_semaphore()
    for step in range(1, N):
        for device in (at_y((y + step) % N), at_x((x + step) % N), at_z((z + step) % N)):
            pl.semaphore_signal(barrier, inc=1, device_id=device, device_id_type=MESH)
    pl.semaphore_signal(barrier, inc=1, device_id=twin, device_id_type=MESH)

    load_rows = pltpu.make_async_copy(rows_hbm.at[0], rows, local_sem.at[0])
    load_merger = pltpu.make_async_copy(merger_hbm.at[0], merger, local_sem.at[1])
    load_before = pltpu.make_async_copy(before_hbm.at[0], before, local_sem.at[2])
    load_rows.start()
    load_merger.start()
    load_before.start()

    load_rows.wait()
    base = (x // PROMPT_X) * SLOTS
    row_ids = lax.broadcasted_iota(jnp.int32, (SLOTS, SLOTS), 0)
    picker = (jnp.broadcast_to(dest_ref[...] - base, (SLOTS, SLOTS)) == row_ids).astype(jnp.float32).astype(jnp.bfloat16)
    for block in range(N):
        placed = jnp.dot(
            picker, rows[:, block * N * LANES : (block + 1) * N * LANES], preferred_element_type=jnp.float32
        ).astype(jnp.bfloat16)
        for part in range(N):
            slot_send[part, block] = placed[:, part * LANES : (part + 1) * LANES]

    pl.semaphore_wait(barrier, 3 * (N - 1) + 1)

    def slot_copy(target, source):
        return remote(slot_send.at[target], slot_recv.at[source], slot_s.at[target], slot_r.at[source], at_y(target))

    for step in range(1, N):
        slot_copy((y + step) % N, y).start()

    half = N // 2
    sender = y // half == core

    def w_block(zz, first, count):
        return weights.at[pl.ds(first, count), pl.ds(pl.multiple_of(zz * UNITS, 16), UNITS), :]

    def wy_copy(target, source):
        return remote(
            w_hbm.at[pl.ds(pl.multiple_of(z * PAIR + target * UNITS, 16), UNITS), :],
            weights.at[source, pl.ds(pl.multiple_of(z * UNITS, 16), UNITS), :],
            wy_s.at[target], wy_r.at[source], at_y(target),
        )

    own_w = pltpu.make_async_copy(
        w_hbm.at[pl.ds(pl.multiple_of(z * PAIR + y * UNITS, 16), UNITS), :],
        weights.at[y, pl.ds(pl.multiple_of(z * UNITS, 16), UNITS), :],
        local_sem.at[3],
    )

    @pl.when(sender)
    def _():
        own_w.start()
        for step in range(1, N):
            wy_copy((y + step) % N, y).start()

    load_merger.wait()

    def shift_inputs(block, carry):
        first = pl.multiple_of(block * PAIR, LANES)
        value = merger[:, pl.ds(first, PAIR)].astype(jnp.float32)
        inputs[0, block] = value[:, :PADDED].astype(jnp.bfloat16)
        inputs[1, block] = pltpu.roll(value, OWN, 1)[:, :PADDED].astype(jnp.bfloat16)
        return carry

    lax.fori_loop(0, N, shift_inputs, 0)
    swap_inputs = remote(inputs.at[1 - core], other_inputs, core_s.at[0], core_r.at[0], twin)
    swap_inputs.start()

    @pl.when(sender)
    def _():
        own_w.wait()

    for step in range(half):
        source = core * half + step

        @pl.when(source != y)
        def _():
            wy_copy(source, source).wait_recv()

    def wz_copy(target, source):
        return remote(
            w_block(source, core * half, half), w_block(source, core * half, half),
            wz_s.at[target], wz_r.at[source], at_z(target),
        )

    def wc_copy(source, owner):
        return remote(
            w_block(source, owner * half, half), w_block(source, owner * half, half),
            wc_s.at[source], wc_r.at[source], twin,
        )

    for step in range(1, N):
        wz_copy((z + step) % N, z).start()
    wc_copy(z, core).start()

    load_before.wait()

    def activate(block, carry):
        first = pl.multiple_of(block * PAIR, LANES)
        value = gelu(before[:, pl.ds(first, PAIR)].astype(jnp.float32))
        hidden[0, block] = value[:, :PADDED].astype(jnp.bfloat16)
        hidden[1, block] = pltpu.roll(value, OWN, 1)[:, :PADDED].astype(jnp.bfloat16)
        return carry

    lax.fori_loop(0, N, activate, 0)
    swap_hidden = remote(hidden.at[1 - core], other_hidden, core_s.at[1], core_r.at[1], twin)
    swap_hidden.start()

    limit = before.shape[1] - 2 * LANES
    first = jnp.minimum((roll * UNITS) // LANES * LANES, limit)
    offset = roll * UNITS - first
    window = before[:, pl.ds(pl.multiple_of(first, LANES), 2 * LANES)]
    ids = lax.broadcasted_iota(jnp.int32, (UNITS, 2 * LANES), 1) - lax.broadcasted_iota(
        jnp.int32, (UNITS, 2 * LANES), 0
    )
    select = (ids == offset).astype(jnp.float32).astype(jnp.bfloat16)
    own_before = lax.dot_general(select, window, (((1,), (1,)), ((), ())), preferred_element_type=jnp.float32)
    slope = gelu_slope(own_before)

    total = slot_send[y].astype(jnp.float32)
    for step in range(1, N):
        source = (y + N - step) % N
        slot_copy(source, source).wait_recv()
        total = total + slot_recv[source].astype(jnp.float32)
    part_send[...] = total.astype(jnp.bfloat16)

    def part_copy(target, source):
        return remote(part_send.at[target], part_recv.at[source], part_s.at[target], part_r.at[source], at_x(target))

    for step in range(1, N):
        part_copy((x + step) % N, x).start()
    part_recv[x] = part_send[x]
    for step in range(1, N):
        source = (x + N - step) % N
        part_copy(source, source).wait_recv()
    parts = part_recv[...].astype(jnp.float32).reshape(N // PROMPT_X, PROMPT_X, SLOTS, LANES)
    merged = (parts[:, 0] + parts[:, 1]).reshape(MERGED, LANES)
    gathered[y] = merged.astype(jnp.bfloat16)

    def gather_copy(target, source):
        return remote(gathered.at[source], gathered.at[source], gather_s.at[target], gather_r.at[source], at_y(target))

    for step in range(1, N):
        gather_copy((y + step) % N, y).start()
    swap_merged = remote(gathered.at[y], other_merged, core_s.at[2], core_r.at[2], twin)
    swap_merged.start()

    for step in range(1, N):
        source = (z + N - step) % N
        wz_copy(source, source).wait_recv()
        wc_copy(source, core).start()

    def term_copy(target, source):
        return remote(term_send.at[target], term_recv.at[source], term_s.at[target], term_r.at[source], at_z(target))

    merged_t = merged.T.astype(jnp.bfloat16)
    swap_merged.wait_recv()
    other_t = other_merged[...].astype(jnp.float32).T.astype(jnp.bfloat16)
    swap_hidden.wait_recv()

    def second_term(target):
        return jnp.dot(merged_t, hidden[core, target], preferred_element_type=jnp.float32) + jnp.dot(
            other_t, other_hidden[target], preferred_element_type=jnp.float32
        )

    for step in range(1, N):
        target = (z + step) % N
        term_send[target] = second_term(target).astype(jnp.bfloat16)
        term_copy(target, z).start()
    second_total = second_term(z)

    for step in range(1, N):
        source = (y + N - step) % N
        gather_copy(source, source).wait_recv()
    for source in range(N):
        wc_copy(source, 1 - core).wait_recv()
    all_merged = jnp.concatenate([gathered[k] for k in range(N)], axis=1)

    def unit_copy(target, source):
        return remote(
            unit_send.at[target], unit_recv.at[source], unit_s.at[target], unit_r.at[source], at_x(target)
        )

    for block in range(0, N, 2):
        wide = jnp.concatenate([weights[k, block * UNITS : (block + 2) * UNITS, :] for k in range(N)], axis=1)
        units = lax.dot_general(wide, all_merged, (((1,), (1,)), ((), ())), preferred_element_type=jnp.float32)
        for k in range(2):
            unit_send[block + k] = units[k * UNITS : (k + 1) * UNITS].astype(jnp.bfloat16)

            @pl.when(x != block + k)
            def _():
                unit_copy(block + k, x).start()

    units = unit_send[x].astype(jnp.float32)
    for step in range(1, N):
        source = (x + N - step) % N
        unit_copy(source, source).wait_recv()
        units = units + unit_recv[source].astype(jnp.float32)
    grads = (units * slope).astype(jnp.bfloat16)
    own_pre[...] = grads
    pre_ref[...] = grads
    swap_pre = remote(own_pre, other_pre, core_s.at[3], core_r.at[3], twin)
    swap_pre.start()

    def last_copy(target, source):
        return remote(last_send.at[target], last_recv.at[source], last_s.at[target], last_r.at[source], at_z(target))

    swap_inputs.wait_recv()
    swap_pre.wait_recv()
    other_grads = other_pre[...]

    def first_term(target):
        return jnp.dot(grads, inputs[core, target], preferred_element_type=jnp.float32) + jnp.dot(
            other_grads, other_inputs[target], preferred_element_type=jnp.float32
        )

    for step in range(1, N):
        target = (z + step) % N
        last_send[target] = first_term(target).astype(jnp.bfloat16)
        last_copy(target, z).start()
    first_total = first_term(z)

    for step in range(1, N):
        source = (z + N - step) % N
        term_copy(source, source).wait_recv()
        second_total = second_total + term_recv[source].astype(jnp.float32)
    second_ref[...] = (second_total * factor).T[:OWN]

    for step in range(1, N):
        source = (z + N - step) % N
        last_copy(source, source).wait_recv()
        first_total = first_total + last_recv[source].astype(jnp.float32)
    first_ref[...] = (first_total * factor)[:, :OWN]

    for step in range(1, N):
        slot_copy((y + step) % N, y).wait_send()
        part_copy((x + step) % N, x).wait_send()
        gather_copy((y + step) % N, y).wait_send()
        wz_copy((z + step) % N, z).wait_send()
        unit_copy((x + step) % N, x).wait_send()
        term_copy((z + step) % N, z).wait_send()
        last_copy((z + step) % N, z).wait_send()
    for source in range(N):
        wc_copy(source, core).wait_send()

    @pl.when(sender)
    def _():
        for step in range(1, N):
            wy_copy((y + step) % N, y).wait_send()

    for copy in (swap_inputs, swap_hidden, swap_merged, swap_pre):
        copy.wait_send()


def body(row_grads, row_dest, merger_in, hidden_pre, w_second):
    factor = 1.0 / math.sqrt(merger_in.shape[1] * lax.axis_size("enc"))
    width = merger_in.shape[2]
    bf16 = jnp.bfloat16
    vmem = pl.BlockSpec(memory_space=pltpu.VMEM)
    hbm = pl.BlockSpec(memory_space=pl.ANY)
    sems = pltpu.SemaphoreType.DMA
    pre, first, second = pl.pallas_call(
        functools.partial(kernel, factor),
        out_shape=(
            jax.ShapeDtypeStruct((UNITS, MERGED), bf16),
            jax.ShapeDtypeStruct((UNITS, OWN), jnp.float32),
            jax.ShapeDtypeStruct((OWN, LANES), jnp.float32),
        ),
        in_specs=[hbm, vmem, hbm, hbm, hbm],
        out_specs=(vmem, vmem, vmem),
        scratch_shapes=[
            pltpu.VMEM((SLOTS, N * N * LANES), bf16),
            pltpu.VMEM((MERGED, width), bf16),
            pltpu.VMEM((MERGED, width), bf16),
            pltpu.VMEM((N, N, SLOTS, LANES), bf16),
            pltpu.VMEM((N, N, SLOTS, LANES), bf16),
            pltpu.VMEM((N, SLOTS, LANES), bf16),
            pltpu.VMEM((N, SLOTS, LANES), bf16),
            pltpu.VMEM((N, MERGED, LANES), bf16),
            pltpu.VMEM((MERGED, LANES), bf16),
            pltpu.VMEM((N, PAIR, LANES), bf16),
            pltpu.VMEM((2, N, MERGED, PADDED), bf16),
            pltpu.VMEM((N, MERGED, PADDED), bf16),
            pltpu.VMEM((2, N, MERGED, PADDED), bf16),
            pltpu.VMEM((N, MERGED, PADDED), bf16),
            pltpu.VMEM((N, LANES, PADDED), bf16),
            pltpu.VMEM((N, LANES, PADDED), bf16),
            pltpu.VMEM((N, UNITS, MERGED), bf16),
            pltpu.VMEM((N, UNITS, MERGED), bf16),
            pltpu.VMEM((UNITS, MERGED), bf16),
            pltpu.VMEM((UNITS, MERGED), bf16),
            pltpu.VMEM((N, UNITS, PADDED), bf16),
            pltpu.VMEM((N, UNITS, PADDED), bf16),
            sems((4,)),
        ]
        + [sems((N,)) for _ in range(18)]
        + [sems((4,)), sems((4,))],
        compiler_params=pltpu.CompilerParams(
            collective_id=0, has_side_effects=True, vmem_limit_bytes=48 * 1024 * 1024
        ),
    )(row_grads, row_dest, merger_in, hidden_pre, w_second)
    return pre.T[None], first.T, second


def solution(mesh):
    return jax.shard_map(
        body,
        mesh=mesh,
        in_specs=(
            P("enc", "roll", None),
            P("enc", "roll"),
            P("enc", None, None),
            P("enc", None, None),
            P(None, "roll"),
        ),
        out_specs=(P("enc", None, "roll"), P("enc", "roll"), P("enc", "roll")),
        check_vma=False,
    )
```

```python
import functools
import math

import jax
import jax.numpy as jnp
from jax import lax
from jax.experimental import pallas as pl
from jax.experimental.pallas import tpu as pltpu
from jax.sharding import PartitionSpec as P

MESH = pl.DeviceIdType.MESH
inv_root_two = 1.0 / math.sqrt(2.0)
inv_root_two_pi = 1.0 / math.sqrt(2.0 * math.pi)
N = 8
SLOTS = 32
LANES = 128
MERGED = 128
UNITS = 80
OWN = 320
PAIR = 640
PADDED = 384
SHARE = MERGED // N
PROMPT_X = 2


def gelu(v):
    return v * (0.5 * (1.0 + lax.erf(v * inv_root_two)))


def gelu_slope(v):
    return 0.5 * (1.0 + lax.erf(v * inv_root_two)) + v * jnp.exp(-0.5 * v * v) * inv_root_two_pi


def kernel(
    factor,
    rows_hbm, dest_ref, merger_hbm, before_hbm, w_hbm,
    pre_ref, first_ref, second_ref,
    rows, merger, before, slot_send, slot_recv, part_send, part_recv, gathered, other_merged,
    weights, hidden, other_hidden, pack_own, pack_swap, pack_other, pack_send, inputs, term_send, term_recv,
    unit_send, unit_recv, pres,
    local_sem, slot_s, slot_r, part_s, part_r, gather_s, gather_r, wy_s, wy_r, wz_s, wz_r, wc_s, wc_r,
    pz_s, pz_r, up_s, up_r, down_s, down_r, unit_s, unit_r, term_s, term_r, pre_s, pre_r, pt_s, pt_r, core_s, core_r,
):
    enc = lax.axis_index("enc")
    roll = lax.axis_index("roll")
    z, core = enc // 2, enc % 2
    x, y = roll // N, roll % N

    def at_y(other):
        return (enc, x * N + other)

    def at_x(other):
        return (enc, other * N + y)

    def at_z(other):
        return (other * 2 + core, roll)

    twin = (z * 2 + (1 - core), roll)

    def remote(src, dst, send, recv, device):
        return pltpu.make_async_remote_copy(
            src_ref=src, dst_ref=dst, send_sem=send, recv_sem=recv, device_id=device, device_id_type=MESH
        )

    barrier = pltpu.get_barrier_semaphore()
    for step in range(1, N):
        for device in (at_y((y + step) % N), at_x((x + step) % N), at_z((z + step) % N)):
            pl.semaphore_signal(barrier, inc=1, device_id=device, device_id_type=MESH)
    pl.semaphore_signal(barrier, inc=1, device_id=twin, device_id_type=MESH)

    load_rows = pltpu.make_async_copy(rows_hbm.at[0], rows, local_sem.at[0])
    share = pl.ds(pl.multiple_of(x * SHARE, SHARE), SHARE)
    load_merger = pltpu.make_async_copy(merger_hbm.at[0, share, :], merger, local_sem.at[1])
    load_before = pltpu.make_async_copy(before_hbm.at[0], before, local_sem.at[2])
    load_rows.start()
    load_merger.start()
    load_before.start()

    pl.semaphore_wait(barrier, 3 * (N - 1) + 1)

    half = N // 2
    sender = y // half == core

    def w_block(zz, first, count):
        return weights.at[pl.ds(first, count), pl.ds(pl.multiple_of(zz * UNITS, 16), UNITS), :]

    def wy_copy(target, source):
        return remote(
            w_hbm.at[pl.ds(pl.multiple_of(z * PAIR + target * UNITS, 16), UNITS), :],
            weights.at[source, pl.ds(pl.multiple_of(z * UNITS, 16), UNITS), :],
            wy_s.at[target], wy_r.at[source], at_y(target),
        )

    own_w = pltpu.make_async_copy(
        w_hbm.at[pl.ds(pl.multiple_of(z * PAIR + y * UNITS, 16), UNITS), :],
        weights.at[y, pl.ds(pl.multiple_of(z * UNITS, 16), UNITS), :],
        local_sem.at[3],
    )

    @pl.when(sender)
    def _():
        own_w.start()
        for step in range(1, N):
            wy_copy((y + step) % N, y).start()

    load_rows.wait()
    base = (x // PROMPT_X) * SLOTS
    row_ids = lax.broadcasted_iota(jnp.int32, (SLOTS, SLOTS), 0)
    picker = (jnp.broadcast_to(dest_ref[...] - base, (SLOTS, SLOTS)) == row_ids).astype(jnp.float32).astype(jnp.bfloat16)
    for block in range(N):
        placed = jnp.dot(
            picker, rows[:, block * N * LANES : (block + 1) * N * LANES], preferred_element_type=jnp.float32
        ).astype(jnp.bfloat16)
        for part in range(N):
            slot_send[part, block] = placed[:, part * LANES : (part + 1) * LANES]

    def slot_copy(target, source):
        return remote(slot_send.at[target], slot_recv.at[source], slot_s.at[target], slot_r.at[source], at_y(target))

    for step in range(1, N):
        slot_copy((y + step) % N, y).start()

    load_merger.wait()
    for block in range(N):
        value = merger[:, block * PAIR : (block + 1) * PAIR]
        pack_own[block] = value
        pack_swap[block] = pltpu.roll(value.astype(jnp.float32), OWN, 1).astype(jnp.bfloat16)
    swap_inputs = remote(pack_swap, pack_other, core_s.at[0], core_r.at[0], twin)
    swap_inputs.start()

    load_before.wait()

    def activate(block, carry):
        first = pl.multiple_of(block * PAIR, LANES)
        value = gelu(before[:, pl.ds(first, PAIR)].astype(jnp.float32))
        hidden[0, block] = value[:, :PADDED].astype(jnp.bfloat16)
        hidden[1, block] = pltpu.roll(value, OWN, 1)[:, :PADDED].astype(jnp.bfloat16)
        return carry

    lax.fori_loop(0, N // 2, activate, 0)

    swap_inputs.wait_recv()
    lane_core = lax.broadcasted_iota(jnp.int32, (SHARE, PAIR), 1) // OWN
    for block in range(N):
        pack_send[block] = jnp.where(
            lane_core == core, pack_own[block].astype(jnp.float32), pack_other[block].astype(jnp.float32)
        ).astype(jnp.bfloat16)

    def pz_copy(target, source):
        return remote(
            pack_send.at[target], inputs.at[source, share, :], pz_s.at[target], pz_r.at[source], at_z(target)
        )

    for step in range(1, N):
        pz_copy((z + step) % N, z).start()
    inputs[z, share, :] = pack_send[z]

    @pl.when(sender)
    def _():
        own_w.wait()

    for step in range(half):
        source = core * half + step

        @pl.when(source != y)
        def _():
            wy_copy(source, source).wait_recv()

    def wz_copy(target, source):
        return remote(
            w_block(source, core * half, half), w_block(source, core * half, half),
            wz_s.at[target], wz_r.at[source], at_z(target),
        )

    def wc_copy(source, owner):
        return remote(
            w_block(source, owner * half, half), w_block(source, owner * half, half),
            wc_s.at[source], wc_r.at[source], twin,
        )

    for step in range(1, N):
        wz_copy((z + step) % N, z).start()
    wc_copy(z, core).start()

    lax.fori_loop(N // 2, N, activate, 0)
    swap_hidden = remote(hidden.at[1 - core], other_hidden, core_s.at[1], core_r.at[1], twin)
    swap_hidden.start()

    for step in range(1, N):
        source = (z + N - step) % N
        pz_copy(source, source).wait_recv()

    def block_of(owner):
        return inputs.at[:, pl.ds(pl.multiple_of(owner * SHARE, SHARE), SHARE), :]

    def up_copy(step):
        owner = (x + N - step) % N
        return remote(block_of(owner), block_of(owner), up_s.at[step], up_r.at[step], at_x((x + 1) % N))

    def down_copy(step):
        owner = (x + step) % N
        return remote(block_of(owner), block_of(owner), down_s.at[step], down_r.at[step], at_x((x + N - 1) % N))

    def up_arrival(step):
        owner = (x + N - step - 1) % N
        return remote(block_of(owner), block_of(owner), up_s.at[step], up_r.at[step], at_x((x + 1) % N))

    def down_arrival(step):
        owner = (x + step + 1) % N
        return remote(block_of(owner), block_of(owner), down_s.at[step], down_r.at[step], at_x((x + N - 1) % N))

    def pass_on(step):
        if step:
            up_arrival(step - 1).wait_recv()
            down_arrival(step - 1).wait_recv()
        up_copy(step).start()
        if step < half - 1:
            down_copy(step).start()

    pass_on(0)

    limit = before.shape[1] - 2 * LANES
    first = jnp.minimum((roll * UNITS) // LANES * LANES, limit)
    offset = roll * UNITS - first
    window = before[:, pl.ds(pl.multiple_of(first, LANES), 2 * LANES)]
    ids = lax.broadcasted_iota(jnp.int32, (UNITS, 2 * LANES), 1) - lax.broadcasted_iota(
        jnp.int32, (UNITS, 2 * LANES), 0
    )
    select = (ids == offset).astype(jnp.float32).astype(jnp.bfloat16)
    own_before = lax.dot_general(select, window, (((1,), (1,)), ((), ())), preferred_element_type=jnp.float32)
    slope = gelu_slope(own_before)

    total = slot_send[y].astype(jnp.float32)
    for step in range(1, N):
        source = (y + N - step) % N
        slot_copy(source, source).wait_recv()
        total = total + slot_recv[source].astype(jnp.float32)
    part_send[...] = total.astype(jnp.bfloat16)

    def part_copy(target, source):
        return remote(part_send.at[target], part_recv.at[source], part_s.at[target], part_r.at[source], at_x(target))

    for step in range(1, N):
        part_copy((x + step) % N, x).start()
    pass_on(1)
    part_recv[x] = part_send[x]
    for step in range(1, N):
        source = (x + N - step) % N
        part_copy(source, source).wait_recv()
    parts = part_recv[...].astype(jnp.float32).reshape(N // PROMPT_X, PROMPT_X, SLOTS, LANES)
    merged = (parts[:, 0] + parts[:, 1]).reshape(MERGED, LANES)
    gathered[y] = merged.astype(jnp.bfloat16)

    def gather_copy(target, source):
        return remote(gathered.at[source], gathered.at[source], gather_s.at[target], gather_r.at[source], at_y(target))

    for step in range(1, N):
        gather_copy((y + step) % N, y).start()
    swap_merged = remote(gathered.at[y], other_merged, core_s.at[2], core_r.at[2], twin)
    swap_merged.start()

    def term_copy(target, source):
        return remote(term_send.at[target], term_recv.at[source], term_s.at[target], term_r.at[source], at_z(target))

    merged_t = merged.T.astype(jnp.bfloat16)
    swap_merged.wait_recv()
    other_t = other_merged[...].astype(jnp.float32).T.astype(jnp.bfloat16)
    swap_hidden.wait_recv()

    rest = PADDED - OWN
    low_lanes = lax.broadcasted_iota(jnp.int32, (LANES // 2, LANES), 1) < LANES - rest

    def second_term(target):
        term = jnp.dot(merged_t, hidden[core, target], preferred_element_type=jnp.float32) + jnp.dot(
            other_t, other_hidden[target], preferred_element_type=jnp.float32
        )
        upper = term[: LANES // 2]
        lower = pltpu.roll(term[LANES // 2 :], rest, 1)
        shared = jnp.where(low_lanes, upper[:, PADDED - LANES :], lower[:, :LANES])
        return jnp.concatenate([upper[:, : PADDED - LANES], shared, lower[:, LANES:]], axis=1)

    for step in range(1, N):
        target = (z + step) % N
        term_send[target] = second_term(target).astype(jnp.bfloat16)
        term_copy(target, z).start()
        source = (z + N - step) % N
        wz_copy(source, source).wait_recv()
        wc_copy(source, core).start()
    second_total = second_term(z)
    pass_on(2)

    for step in range(1, N):
        source = (y + N - step) % N
        gather_copy(source, source).wait_recv()
    for source in range(N):
        wc_copy(source, 1 - core).wait_recv()
    all_merged = jnp.concatenate([gathered[k] for k in range(N)], axis=1)

    def unit_copy(target, source):
        return remote(
            unit_send.at[target], unit_recv.at[source], unit_s.at[target], unit_r.at[source], at_x(target)
        )

    for block in range(0, N, 2):
        wide = jnp.concatenate([weights[k, block * UNITS : (block + 2) * UNITS, :] for k in range(N)], axis=1)
        units = lax.dot_general(wide, all_merged, (((1,), (1,)), ((), ())), preferred_element_type=jnp.float32)
        for k in range(2):
            unit_send[block + k] = units[k * UNITS : (k + 1) * UNITS].astype(jnp.bfloat16)

            @pl.when(x != block + k)
            def _():
                unit_copy(block + k, x).start()

    pass_on(3)
    units = unit_send[x].astype(jnp.float32)
    for step in range(1, N):
        source = (x + N - step) % N
        unit_copy(source, source).wait_recv()
        units = units + unit_recv[source].astype(jnp.float32)
    grads = (units * slope).astype(jnp.bfloat16)
    pres[core, z] = grads
    pre_ref[...] = grads

    def pre_copy(target, source):
        return remote(
            pres.at[core, source], pres.at[core, source], pre_s.at[target], pre_r.at[source], at_z(target)
        )

    def pt_copy(source, owner):
        return remote(pres.at[owner, source], pres.at[owner, source], pt_s.at[source], pt_r.at[source], twin)

    for step in range(1, N):
        pre_copy((z + step) % N, z).start()
    pt_copy(z, core).start()
    for step in range(1, N):
        source = (z + N - step) % N
        pre_copy(source, source).wait_recv()
        pt_copy(source, core).start()

    for step in range(1, N):
        source = (z + N - step) % N
        term_copy(source, source).wait_recv()
        second_total = second_total + term_recv[source].astype(jnp.float32)
    second_total = second_total * factor
    second_ref[:, : LANES // 2] = second_total[:, :PADDED].T[:OWN]
    second_ref[:, LANES // 2 :] = pltpu.roll(second_total[:, PAIR - PADDED :], OWN, 1).T[:OWN]

    up_arrival(half - 1).wait_recv()
    for source in range(N):
        pt_copy(source, 1 - core).wait_recv()
    width = N * MERGED
    low = jnp.dot(
        jnp.concatenate([pres[0, k] for k in range(N)], axis=1),
        inputs[:, :, :PADDED].reshape(width, PADDED),
        preferred_element_type=jnp.float32,
    )
    high = jnp.dot(
        jnp.concatenate([pres[1, k] for k in range(N)], axis=1),
        inputs[:, :, PAIR - PADDED :].reshape(width, PADDED),
        preferred_element_type=jnp.float32,
    )
    first_ref[...] = ((low + pltpu.roll(high, OWN, 1)) * factor)[:, :OWN]

    for step in range(1, N):
        slot_copy((y + step) % N, y).wait_send()
        part_copy((x + step) % N, x).wait_send()
        gather_copy((y + step) % N, y).wait_send()
        wz_copy((z + step) % N, z).wait_send()
        unit_copy((x + step) % N, x).wait_send()
        term_copy((z + step) % N, z).wait_send()
        pre_copy((z + step) % N, z).wait_send()
        pz_copy((z + step) % N, z).wait_send()
    for step in range(half):
        up_copy(step).wait_send()
    for step in range(half - 1):
        down_copy(step).wait_send()
    for source in range(N):
        wc_copy(source, core).wait_send()
        pt_copy(source, core).wait_send()

    @pl.when(sender)
    def _():
        for step in range(1, N):
            wy_copy((y + step) % N, y).wait_send()

    for copy in (swap_inputs, swap_hidden, swap_merged):
        copy.wait_send()


def body(row_grads, row_dest, merger_in, hidden_pre, w_second):
    factor = 1.0 / math.sqrt(merger_in.shape[1] * lax.axis_size("enc"))
    width = merger_in.shape[2]
    bf16 = jnp.bfloat16
    vmem = pl.BlockSpec(memory_space=pltpu.VMEM)
    hbm = pl.BlockSpec(memory_space=pl.ANY)
    sems = pltpu.SemaphoreType.DMA
    pre, first, second = pl.pallas_call(
        functools.partial(kernel, factor),
        out_shape=(
            jax.ShapeDtypeStruct((UNITS, MERGED), bf16),
            jax.ShapeDtypeStruct((UNITS, OWN), jnp.float32),
            jax.ShapeDtypeStruct((OWN, LANES), jnp.float32),
        ),
        in_specs=[hbm, vmem, hbm, hbm, hbm],
        out_specs=(vmem, vmem, vmem),
        scratch_shapes=[
            pltpu.VMEM((SLOTS, N * N * LANES), bf16),
            pltpu.VMEM((SHARE, width), bf16),
            pltpu.VMEM((MERGED, width), bf16),
            pltpu.VMEM((N, N, SLOTS, LANES), bf16),
            pltpu.VMEM((N, N, SLOTS, LANES), bf16),
            pltpu.VMEM((N, SLOTS, LANES), bf16),
            pltpu.VMEM((N, SLOTS, LANES), bf16),
            pltpu.VMEM((N, MERGED, LANES), bf16),
            pltpu.VMEM((MERGED, LANES), bf16),
            pltpu.VMEM((N, PAIR, LANES), bf16),
            pltpu.VMEM((2, N, MERGED, PADDED), bf16),
            pltpu.VMEM((N, MERGED, PADDED), bf16),
            pltpu.VMEM((N, SHARE, PAIR), bf16),
            pltpu.VMEM((N, SHARE, PAIR), bf16),
            pltpu.VMEM((N, SHARE, PAIR), bf16),
            pltpu.VMEM((N, SHARE, PAIR), bf16),
            pltpu.VMEM((N, MERGED, PAIR), bf16),
            pltpu.VMEM((N, LANES // 2, PAIR), bf16),
            pltpu.VMEM((N, LANES // 2, PAIR), bf16),
            pltpu.VMEM((N, UNITS, MERGED), bf16),
            pltpu.VMEM((N, UNITS, MERGED), bf16),
            pltpu.VMEM((2, N, UNITS, MERGED), bf16),
            sems((4,)),
        ]
        + [sems((N,)) for _ in range(26)]
        + [sems((3,)), sems((3,))],
        compiler_params=pltpu.CompilerParams(
            collective_id=0, has_side_effects=True, vmem_limit_bytes=62 * 1024 * 1024
        ),
    )(row_grads, row_dest, merger_in, hidden_pre, w_second)
    return pre.T[None], first.T, second


def solution(mesh):
    return jax.shard_map(
        body,
        mesh=mesh,
        in_specs=(
            P("enc", "roll", None),
            P("enc", "roll"),
            P("enc", None, None),
            P("enc", None, None),
            P(None, "roll"),
        ),
        out_specs=(P("enc", None, "roll"), P("enc", "roll"), P("enc", "roll")),
        check_vma=False,
    )
```

```python
import functools
import math

import jax
import jax.numpy as jnp
from jax import lax
from jax.experimental import pallas as pl
from jax.experimental.pallas import tpu as pltpu
from jax.sharding import PartitionSpec as P

MESH = pl.DeviceIdType.MESH
inv_root_two = 1.0 / math.sqrt(2.0)
inv_root_two_pi = 1.0 / math.sqrt(2.0 * math.pi)
N = 8
HALF = N // 2
FAR_FIRST = (4, 3, 5, 2, 6, 1, 7)
NEAR_FIRST = (1, 7, 2, 6, 3, 5, 4)
SLOTS = 32
ROWS = SLOTS // 2
LANES = 128
MERGED = 128
UNITS = 80
OWN = 320
PAIR = 640
PADDED = 384
SHARE = MERGED // N
PROMPT_X = 2
PROMPTS = N // PROMPT_X


def gelu(v):
    return v * (0.5 * (1.0 + lax.erf(v * inv_root_two)))


def gelu_slope(v):
    return 0.5 * (1.0 + lax.erf(v * inv_root_two)) + v * jnp.exp(-0.5 * v * v) * inv_root_two_pi


def kernel(
    factor,
    rows_hbm, dest_ref, merger_hbm, before_hbm, w_hbm,
    pre_ref, first_ref, second_ref,
    rows, merger, before, ya_send, ya_recv, yb_send, yb_recv, xa_send, xa_recv, xb_send, xb_recv,
    gathered, other_merged,
    weights, hidden, other_hidden, pack_own, pack_swap, pack_other, pack_send, inputs, term_send, term_recv,
    unit_total, unit_send, unit_recv, pres,
    local_sem, ya_s, ya_r, yb_s, yb_r, xa_s, xa_r, xb_s, xb_r, gather_s, gather_r, wy_s, wy_r,
    wu_s, wu_r, wd_s, wd_r, wc_s, wc_r, pz_s, pz_r, xu_s, xu_r, xd_s, xd_r,
    unit_s, unit_r, term_s, term_r, pre_s, pre_r, pt_s, pt_r, core_s, core_r,
):
    enc = lax.axis_index("enc")
    roll = lax.axis_index("roll")
    z, core = enc // 2, enc % 2
    x, y = roll // N, roll % N

    def at_y(other):
        return (enc, x * N + other)

    def at_x(other):
        return (enc, other * N + y)

    def at_z(other):
        return (other * 2 + core, roll)

    twin = (z * 2 + (1 - core), roll)

    def remote(src, dst, send, recv, device):
        return pltpu.make_async_remote_copy(
            src_ref=src, dst_ref=dst, send_sem=send, recv_sem=recv, device_id=device, device_id_type=MESH
        )

    def ring(block_of, me, at, up_s, up_r, down_s, down_r):
        above, below = at((me + 1) % N), at((me + N - 1) % N)

        def up(step, owner):
            return remote(block_of(owner), block_of(owner), up_s.at[step], up_r.at[step], above)

        def down(step, owner):
            return remote(block_of(owner), block_of(owner), down_s.at[step], down_r.at[step], below)

        def send(step):
            up(step, (me + N - step) % N).start()
            if step < HALF - 1:
                down(step, (me + step) % N).start()

        def receive(step):
            owners = [(me + N - step - 1) % N]
            up(step, owners[0]).wait_recv()
            if step < HALF - 1:
                owners.append((me + step + 1) % N)
                down(step, owners[1]).wait_recv()
            return owners

        def finish():
            for step in range(HALF):
                up(step, (me + N - step) % N).wait_send()
            for step in range(HALF - 1):
                down(step, (me + step) % N).wait_send()

        return send, receive, finish

    load_rows = pltpu.make_async_copy(rows_hbm.at[0], rows, local_sem.at[0])
    load_rows.start()
    barrier = pltpu.get_barrier_semaphore()
    for step in FAR_FIRST:
        for device in (at_y((y + step) % N), at_x((x + step) % N), at_z((z + step) % N)):
            pl.semaphore_signal(barrier, inc=1, device_id=device, device_id_type=MESH)
    pl.semaphore_signal(barrier, inc=1, device_id=twin, device_id_type=MESH)
    share = pl.ds(pl.multiple_of(x * SHARE, SHARE), SHARE)
    load_merger = pltpu.make_async_copy(merger_hbm.at[0, share, :], merger, local_sem.at[1])
    load_before = pltpu.make_async_copy(before_hbm.at[0], before, local_sem.at[2])
    load_merger.start()
    load_before.start()

    load_rows.wait()
    base = (x // PROMPT_X) * SLOTS
    row_ids = lax.broadcasted_iota(jnp.int32, (SLOTS, SLOTS), 0)
    picker = (jnp.broadcast_to(dest_ref[...] - base, (SLOTS, SLOTS)) == row_ids).astype(jnp.float32).astype(jnp.bfloat16)
    for block in range(N):
        placed = jnp.dot(
            picker, rows[:, block * N * LANES : (block + 1) * N * LANES], preferred_element_type=jnp.float32
        ).astype(jnp.bfloat16)
        xb_send[block] = placed[ROWS:]
        for part in range(N):
            ya_send[part, block] = placed[:ROWS, part * LANES : (part + 1) * LANES]

    pl.semaphore_wait(barrier, 3 * (N - 1) + 1)

    sender = y // HALF == core

    def w_block(zz, owner):
        return weights.at[pl.ds(owner * HALF, HALF), pl.ds(pl.multiple_of(zz * UNITS, 16), UNITS), :]

    def wy_copy(target, source):
        return remote(
            w_hbm.at[pl.ds(pl.multiple_of(z * PAIR + target * UNITS, 16), UNITS), :],
            weights.at[source, pl.ds(pl.multiple_of(z * UNITS, 16), UNITS), :],
            wy_s.at[target], wy_r.at[source], at_y(target),
        )

    own_w = pltpu.make_async_copy(
        w_hbm.at[pl.ds(pl.multiple_of(z * PAIR + y * UNITS, 16), UNITS), :],
        weights.at[y, pl.ds(pl.multiple_of(z * UNITS, 16), UNITS), :],
        local_sem.at[3],
    )

    @pl.when(sender)
    def _():
        own_w.start()
        for step in FAR_FIRST:
            wy_copy((y + step) % N, y).start()

    def ya_copy(target, source):
        return remote(ya_send.at[target], ya_recv.at[source], ya_s.at[target], ya_r.at[source], at_y(target))

    def xb_copy(target, source):
        return remote(xb_send.at[target], xb_recv.at[source], xb_s.at[target], xb_r.at[source], at_x(target))

    for step in FAR_FIRST:
        ya_copy((y + step) % N, y).start()
        xb_copy((x + step) % N, x).start()

    load_merger.wait()
    for block in range(N):
        value = merger[:, block * PAIR : (block + 1) * PAIR]
        pack_own[block] = value
        pack_swap[block] = pltpu.roll(value.astype(jnp.float32), OWN, 1).astype(jnp.bfloat16)
    swap_inputs = remote(pack_swap, pack_other, core_s.at[0], core_r.at[0], twin)
    swap_inputs.start()

    load_before.wait()

    def activate(block, carry):
        first = pl.multiple_of(block * PAIR, LANES)
        value = gelu(before[:, pl.ds(first, PAIR)].astype(jnp.float32))
        hidden[0, block] = value[:, :PADDED].astype(jnp.bfloat16)
        hidden[1, block] = pltpu.roll(value, OWN, 1)[:, :PADDED].astype(jnp.bfloat16)
        return carry

    lax.fori_loop(0, HALF, activate, 0)

    @pl.when(sender)
    def _():
        own_w.wait()

    for step in range(HALF):
        source = core * HALF + step

        @pl.when(source != y)
        def _():
            wy_copy(source, source).wait_recv()

    w_send, w_receive, w_finish = ring(lambda zz: w_block(zz, core), z, at_z, wu_s, wu_r, wd_s, wd_r)

    def wc_copy(source, owner):
        return remote(w_block(source, owner), w_block(source, owner), wc_s.at[source], wc_r.at[source], twin)

    def w_pass_on(step):
        for source in w_receive(step - 1):
            wc_copy(source, core).start()
        if step < HALF:
            w_send(step)

    w_send(0)
    wc_copy(z, core).start()

    swap_inputs.wait_recv()
    lane_core = lax.broadcasted_iota(jnp.int32, (SHARE, PAIR), 1) // OWN
    for block in range(N):
        pack_send[block] = jnp.where(
            lane_core == core, pack_own[block].astype(jnp.float32), pack_other[block].astype(jnp.float32)
        ).astype(jnp.bfloat16)

    def pz_copy(target, source):
        return remote(
            pack_send.at[target], inputs.at[source, share, :], pz_s.at[target], pz_r.at[source], at_z(target)
        )

    for step in FAR_FIRST:
        pz_copy((z + step) % N, z).start()
    inputs[z, share, :] = pack_send[z]
    x_send, x_receive, x_finish = ring(
        lambda owner: inputs.at[:, pl.ds(pl.multiple_of(owner * SHARE, SHARE), SHARE), :],
        x, at_x, xu_s, xu_r, xd_s, xd_r,
    )

    lax.fori_loop(HALF, N, activate, 0)
    swap_hidden = remote(hidden.at[1 - core], other_hidden, core_s.at[1], core_r.at[1], twin)
    swap_hidden.start()
    w_pass_on(1)

    limit = before.shape[1] - 2 * LANES
    first = jnp.minimum((roll * UNITS) // LANES * LANES, limit)
    offset = roll * UNITS - first
    window = before[:, pl.ds(pl.multiple_of(first, LANES), 2 * LANES)]
    ids = lax.broadcasted_iota(jnp.int32, (UNITS, 2 * LANES), 1) - lax.broadcasted_iota(
        jnp.int32, (UNITS, 2 * LANES), 0
    )
    select = (ids == offset).astype(jnp.float32).astype(jnp.bfloat16)
    own_before = lax.dot_general(select, window, (((1,), (1,)), ((), ())), preferred_element_type=jnp.float32)
    slope = gelu_slope(own_before)

    def yb_copy(target, source):
        return remote(yb_send.at[target], yb_recv.at[source], yb_s.at[target], yb_r.at[source], at_y(target))

    def xa_copy(target, source):
        return remote(xa_send.at[target], xa_recv.at[source], xa_s.at[target], xa_r.at[source], at_x(target))

    for step in NEAR_FIRST:
        source = (x + step) % N
        xb_copy(source, source).wait_recv()
    xb_recv[x] = xb_send[x]
    for prompt in range(PROMPTS):
        total = xb_recv[PROMPT_X * prompt].astype(jnp.float32) + xb_recv[PROMPT_X * prompt + 1].astype(jnp.float32)
        for part in range(N):
            yb_send[part, prompt] = total[:, part * LANES : (part + 1) * LANES].astype(jnp.bfloat16)

    total = ya_send[y].astype(jnp.float32)
    for step in NEAR_FIRST:
        source = (y + step) % N
        ya_copy(source, source).wait_recv()
        total = total + ya_recv[source].astype(jnp.float32)
    xa_send[...] = total.astype(jnp.bfloat16)
    for step in FAR_FIRST:
        yb_copy((y + step) % N, y).start()
        xa_copy((x + step) % N, x).start()
    xa_recv[x] = xa_send[x]

    for step in NEAR_FIRST:
        source = (z + step) % N
        pz_copy(source, source).wait_recv()
    x_send(0)
    w_pass_on(2)

    lower = yb_send[y].astype(jnp.float32)
    for step in NEAR_FIRST:
        source = (y + step) % N
        yb_copy(source, source).wait_recv()
        lower = lower + yb_recv[source].astype(jnp.float32)
    for step in NEAR_FIRST:
        source = (x + step) % N
        xa_copy(source, source).wait_recv()
    parts = xa_recv[...].astype(jnp.float32).reshape(PROMPTS, PROMPT_X, ROWS, LANES)
    upper = parts[:, 0] + parts[:, 1]
    merged = jnp.concatenate([upper, lower], axis=1).reshape(MERGED, LANES)
    gathered[y] = merged.astype(jnp.bfloat16)

    def gather_copy(target, source):
        return remote(gathered.at[source], gathered.at[source], gather_s.at[target], gather_r.at[source], at_y(target))

    for step in FAR_FIRST:
        gather_copy((y + step) % N, y).start()
    swap_merged = remote(gathered.at[y], other_merged, core_s.at[2], core_r.at[2], twin)
    swap_merged.start()
    w_pass_on(3)
    x_receive(0)
    x_send(1)

    def term_copy(target, source):
        return remote(term_send.at[target], term_recv.at[source], term_s.at[target], term_r.at[source], at_z(target))

    merged_t = merged.T.astype(jnp.bfloat16)
    swap_merged.wait_recv()
    other_t = other_merged[...].astype(jnp.float32).T.astype(jnp.bfloat16)
    swap_hidden.wait_recv()

    rest = PADDED - OWN
    low_lanes = lax.broadcasted_iota(jnp.int32, (LANES // 2, LANES), 1) < LANES - rest

    def second_term(target):
        term = jnp.dot(merged_t, hidden[core, target], preferred_element_type=jnp.float32) + jnp.dot(
            other_t, other_hidden[target], preferred_element_type=jnp.float32
        )
        top = term[: LANES // 2]
        bottom = pltpu.roll(term[LANES // 2 :], rest, 1)
        shared = jnp.where(low_lanes, top[:, PADDED - LANES :], bottom[:, :LANES])
        return jnp.concatenate([top[:, : PADDED - LANES], shared, bottom[:, LANES:]], axis=1)

    for step in FAR_FIRST:
        target = (z + step) % N
        term_send[target] = second_term(target).astype(jnp.bfloat16)
        term_copy(target, z).start()
    second_total = second_term(z)
    w_pass_on(4)
    x_receive(1)
    x_send(2)

    for source in range(N):
        wc_copy(source, 1 - core).wait_recv()
    order = (0,) + NEAR_FIRST
    for pair in range(HALF):
        sources = [(y + step) % N for step in order[2 * pair : 2 * pair + 2]]
        for step, source in zip(order[2 * pair : 2 * pair + 2], sources):
            if step:
                gather_copy(source, source).wait_recv()
        product = lax.dot_general(
            jnp.concatenate([weights[source] for source in sources], axis=1),
            jnp.concatenate([gathered[source] for source in sources], axis=1),
            (((1,), (1,)), ((), ())),
            preferred_element_type=jnp.float32,
        )
        if pair == 0:
            unit_total[...] = product
        elif pair < HALF - 1:
            unit_total[...] += product
        else:
            unit_send[...] = (unit_total[...] + product).astype(jnp.bfloat16).reshape(N, UNITS, MERGED)

    def unit_copy(target, source):
        return remote(
            unit_send.at[target], unit_recv.at[source], unit_s.at[target], unit_r.at[source], at_x(target)
        )

    for step in FAR_FIRST:
        unit_copy((x + step) % N, x).start()
    x_receive(2)
    x_send(3)
    units = unit_send[x].astype(jnp.float32)
    for step in NEAR_FIRST:
        source = (x + step) % N
        unit_copy(source, source).wait_recv()
        units = units + unit_recv[source].astype(jnp.float32)
    grads = (units * slope).astype(jnp.bfloat16)
    pres[core, z] = grads
    pre_ref[...] = grads

    def pre_copy(target, source):
        return remote(
            pres.at[core, source], pres.at[core, source], pre_s.at[target], pre_r.at[source], at_z(target)
        )

    def pt_copy(source, owner):
        return remote(pres.at[owner, source], pres.at[owner, source], pt_s.at[source], pt_r.at[source], twin)

    for step in FAR_FIRST:
        pre_copy((z + step) % N, z).start()
    pt_copy(z, core).start()

    for step in NEAR_FIRST:
        source = (z + step) % N
        term_copy(source, source).wait_recv()
        second_total = second_total + term_recv[source].astype(jnp.float32)
    second_total = second_total * factor
    second_ref[:, : LANES // 2] = second_total[:, :PADDED].T[:OWN]
    second_ref[:, LANES // 2 :] = pltpu.roll(second_total[:, PAIR - PADDED :], OWN, 1).T[:OWN]

    for step in NEAR_FIRST:
        source = (z + step) % N
        pre_copy(source, source).wait_recv()
        pt_copy(source, core).start()
    x_receive(3)
    for source in range(N):
        pt_copy(source, 1 - core).wait_recv()
    depth = N * MERGED
    low = jnp.dot(
        jnp.concatenate([pres[0, k] for k in range(N)], axis=1),
        inputs[:, :, :PADDED].reshape(depth, PADDED),
        preferred_element_type=jnp.float32,
    )
    high = jnp.dot(
        jnp.concatenate([pres[1, k] for k in range(N)], axis=1),
        inputs[:, :, PAIR - PADDED :].reshape(depth, PADDED),
        preferred_element_type=jnp.float32,
    )
    first_ref[...] = ((low + pltpu.roll(high, OWN, 1)) * factor)[:, :OWN]

    for step in range(1, N):
        ya_copy((y + step) % N, y).wait_send()
        yb_copy((y + step) % N, y).wait_send()
        xa_copy((x + step) % N, x).wait_send()
        xb_copy((x + step) % N, x).wait_send()
        gather_copy((y + step) % N, y).wait_send()
        unit_copy((x + step) % N, x).wait_send()
        term_copy((z + step) % N, z).wait_send()
        pre_copy((z + step) % N, z).wait_send()
        pz_copy((z + step) % N, z).wait_send()
    w_finish()
    x_finish()
    for source in range(N):
        wc_copy(source, core).wait_send()
        pt_copy(source, core).wait_send()

    @pl.when(sender)
    def _():
        for step in range(1, N):
            wy_copy((y + step) % N, y).wait_send()

    for copy in (swap_inputs, swap_hidden, swap_merged):
        copy.wait_send()


def body(row_grads, row_dest, merger_in, hidden_pre, w_second):
    factor = 1.0 / math.sqrt(merger_in.shape[1] * lax.axis_size("enc"))
    width = merger_in.shape[2]
    bf16 = jnp.bfloat16
    vmem = pl.BlockSpec(memory_space=pltpu.VMEM)
    hbm = pl.BlockSpec(memory_space=pltpu.HBM)
    sems = pltpu.SemaphoreType.DMA
    pre, first, second = pl.pallas_call(
        functools.partial(kernel, factor),
        out_shape=(
            jax.ShapeDtypeStruct((UNITS, MERGED), bf16),
            jax.ShapeDtypeStruct((UNITS, OWN), jnp.float32),
            jax.ShapeDtypeStruct((OWN, LANES), jnp.float32),
        ),
        in_specs=[hbm, vmem, hbm, hbm, hbm],
        out_specs=(vmem, vmem, vmem),
        scratch_shapes=[
            pltpu.VMEM((SLOTS, N * N * LANES), bf16),
            pltpu.VMEM((SHARE, width), bf16),
            pltpu.VMEM((MERGED, width), bf16),
            pltpu.VMEM((N, N, ROWS, LANES), bf16),
            pltpu.VMEM((N, N, ROWS, LANES), bf16),
            pltpu.VMEM((N, PROMPTS, ROWS, LANES), bf16),
            pltpu.VMEM((N, PROMPTS, ROWS, LANES), bf16),
            pltpu.VMEM((N, ROWS, LANES), bf16),
            pltpu.VMEM((N, ROWS, LANES), bf16),
            pltpu.VMEM((N, ROWS, N * LANES), bf16),
            pltpu.VMEM((N, ROWS, N * LANES), bf16),
            pltpu.VMEM((N, MERGED, LANES), bf16),
            pltpu.VMEM((MERGED, LANES), bf16),
            pltpu.VMEM((N, PAIR, LANES), bf16),
            pltpu.VMEM((2, N, MERGED, PADDED), bf16),
            pltpu.VMEM((N, MERGED, PADDED), bf16),
            pltpu.VMEM((N, SHARE, PAIR), bf16),
            pltpu.VMEM((N, SHARE, PAIR), bf16),
            pltpu.VMEM((N, SHARE, PAIR), bf16),
            pltpu.VMEM((N, SHARE, PAIR), bf16),
            pltpu.VMEM((N, MERGED, PAIR), bf16),
            pltpu.VMEM((N, LANES // 2, PAIR), bf16),
            pltpu.VMEM((N, LANES // 2, PAIR), bf16),
            pltpu.VMEM((PAIR, MERGED), jnp.float32),
            pltpu.VMEM((N, UNITS, MERGED), bf16),
            pltpu.VMEM((N, UNITS, MERGED), bf16),
            pltpu.VMEM((2, N, UNITS, MERGED), bf16),
            sems((4,)),
        ]
        + [sems((N,)) for _ in range(12)]
        + [sems((HALF,)) for _ in range(4)]
        + [sems((N,)) for _ in range(4)]
        + [sems((HALF,)) for _ in range(4)]
        + [sems((N,)) for _ in range(8)]
        + [sems((3,)), sems((3,))],
        compiler_params=pltpu.CompilerParams(
            collective_id=0, has_side_effects=True, vmem_limit_bytes=54700 * 1024
        ),
    )(row_grads, row_dest, merger_in, hidden_pre, w_second)
    return pre.T[None], first.T, second


def solution(mesh):
    return jax.shard_map(
        body,
        mesh=mesh,
        in_specs=(
            P("enc", "roll", None),
            P("enc", "roll"),
            P("enc", None, None),
            P("enc", None, None),
            P(None, "roll"),
        ),
        out_specs=(P("enc", None, "roll"), P("enc", "roll"), P("enc", "roll")),
        check_vma=False,
    )
```

```python
import functools
import math

import jax
import jax.numpy as jnp
from jax import lax
from jax.experimental import pallas as pl
from jax.experimental.pallas import tpu as pltpu
from jax.sharding import PartitionSpec as P

MESH = pl.DeviceIdType.MESH
inv_root_two = 1.0 / math.sqrt(2.0)
inv_root_two_pi = 1.0 / math.sqrt(2.0 * math.pi)
N = 8
HALF = N // 2
FAR_FIRST = (4, 3, 5, 2, 6, 1, 7)
NEAR_FIRST = (1, 7, 2, 6, 3, 5, 4)
SLOTS = 32
ROWS = SLOTS // 2
LANES = 128
MERGED = 128
UNITS = 80
OWN = 320
PAIR = 640
PADDED = 384
SHARE = MERGED // N
PROMPT_X = 2
PROMPTS = N // PROMPT_X


def gelu(v):
    return v * (0.5 * (1.0 + lax.erf(v * inv_root_two)))


def gelu_slope(v):
    return 0.5 * (1.0 + lax.erf(v * inv_root_two)) + v * jnp.exp(-0.5 * v * v) * inv_root_two_pi


def kernel(
    factor,
    rows_hbm, dest_ref, merger_hbm, before_hbm, w_hbm,
    pre_ref, first_ref, second_ref,
    rows, merger, before, ya_send, ya_recv, yb_send, yb_recv, xa_send, xa_recv, xb_send, xb_recv,
    gathered, other_merged,
    weights, hidden, other_hidden, pack_own, pack_swap, pack_other, pack_send, inputs, term_send, term_recv,
    unit_total, unit_send, unit_recv, pres,
    local_sem, ya_s, ya_r, yb_s, yb_r, xa_s, xa_r, xb_s, xb_r, gather_s, gather_r, wy_s, wy_r,
    wz_s, wz_r, wc_s, wc_r, pz_s, pz_r, xu_s, xu_r, xd_s, xd_r,
    unit_s, unit_r, term_s, term_r, pre_s, pre_r, pt_s, pt_r, core_s, core_r,
):
    enc = lax.axis_index("enc")
    roll = lax.axis_index("roll")
    z, core = enc // 2, enc % 2
    x, y = roll // N, roll % N

    def at_y(other):
        return (enc, x * N + other)

    def at_x(other):
        return (enc, other * N + y)

    def at_z(other):
        return (other * 2 + core, roll)

    twin = (z * 2 + (1 - core), roll)

    def remote(src, dst, send, recv, device):
        return pltpu.make_async_remote_copy(
            src_ref=src, dst_ref=dst, send_sem=send, recv_sem=recv, device_id=device, device_id_type=MESH
        )

    def ring(block_of, me, at, up_s, up_r, down_s, down_r):
        above, below = at((me + 1) % N), at((me + N - 1) % N)

        def up(step, owner):
            return remote(block_of(owner), block_of(owner), up_s.at[step], up_r.at[step], above)

        def down(step, owner):
            return remote(block_of(owner), block_of(owner), down_s.at[step], down_r.at[step], below)

        def send(step):
            up(step, (me + N - step) % N).start()
            if step < HALF - 1:
                down(step, (me + step) % N).start()

        def receive(step):
            owners = [(me + N - step - 1) % N]
            up(step, owners[0]).wait_recv()
            if step < HALF - 1:
                owners.append((me + step + 1) % N)
                down(step, owners[1]).wait_recv()
            return owners

        def finish():
            for step in range(HALF):
                up(step, (me + N - step) % N).wait_send()
            for step in range(HALF - 1):
                down(step, (me + step) % N).wait_send()

        return send, receive, finish

    load_rows = pltpu.make_async_copy(rows_hbm.at[0], rows, local_sem.at[0])
    load_rows.start()
    barrier = pltpu.get_barrier_semaphore()
    for step in FAR_FIRST:
        for device in (at_y((y + step) % N), at_x((x + step) % N), at_z((z + step) % N)):
            pl.semaphore_signal(barrier, inc=1, device_id=device, device_id_type=MESH)
    pl.semaphore_signal(barrier, inc=1, device_id=twin, device_id_type=MESH)
    share = pl.ds(pl.multiple_of(x * SHARE, SHARE), SHARE)
    load_merger = pltpu.make_async_copy(merger_hbm.at[0, share, :], merger, local_sem.at[1])
    load_before = pltpu.make_async_copy(before_hbm.at[0], before, local_sem.at[2])
    load_merger.start()
    load_before.start()

    pl.semaphore_wait(barrier, 3 * (N - 1) + 1)

    sender = y // HALF == core

    def w_block(zz, owner):
        return weights.at[pl.ds(owner * HALF, HALF), pl.ds(pl.multiple_of(zz * UNITS, 16), UNITS), :]

    def wy_copy(target, source):
        return remote(
            w_hbm.at[pl.ds(pl.multiple_of(z * PAIR + target * UNITS, 16), UNITS), :],
            weights.at[source, pl.ds(pl.multiple_of(z * UNITS, 16), UNITS), :],
            wy_s.at[target], wy_r.at[source], at_y(target),
        )

    own_w = pltpu.make_async_copy(
        w_hbm.at[pl.ds(pl.multiple_of(z * PAIR + y * UNITS, 16), UNITS), :],
        weights.at[y, pl.ds(pl.multiple_of(z * UNITS, 16), UNITS), :],
        local_sem.at[3],
    )

    @pl.when(sender)
    def _():
        own_w.start()
        for step in FAR_FIRST:
            wy_copy((y + step) % N, y).start()

    load_rows.wait()
    base = (x // PROMPT_X) * SLOTS
    row_ids = lax.broadcasted_iota(jnp.int32, (SLOTS, SLOTS), 0)
    picker = (jnp.broadcast_to(dest_ref[...] - base, (SLOTS, SLOTS)) == row_ids).astype(jnp.float32).astype(jnp.bfloat16)
    for block in range(N):
        placed = jnp.dot(
            picker, rows[:, block * N * LANES : (block + 1) * N * LANES], preferred_element_type=jnp.float32
        ).astype(jnp.bfloat16)
        xb_send[block] = placed[ROWS:]
        for part in range(N):
            ya_send[part, block] = placed[:ROWS, part * LANES : (part + 1) * LANES]

    def ya_copy(target, source):
        return remote(ya_send.at[target], ya_recv.at[source], ya_s.at[target], ya_r.at[source], at_y(target))

    def xb_copy(target, source):
        return remote(xb_send.at[target], xb_recv.at[source], xb_s.at[target], xb_r.at[source], at_x(target))

    for step in FAR_FIRST:
        ya_copy((y + step) % N, y).start()
        xb_copy((x + step) % N, x).start()

    @pl.when(sender)
    def _():
        own_w.wait()

    for step in range(HALF):
        source = core * HALF + step

        @pl.when(source != y)
        def _():
            wy_copy(source, source).wait_recv()

    first_hop = ((2, 0), (N - 2, 1), (1, 2), (N - 1, 3))
    second_hop = ((N - 2, 1, 4), (N - 2, 2, 5), (2, N - 1, 6))

    def wz_copy(source, target, send):
        block = w_block(source, core)
        return remote(block, block, wz_s.at[send], wz_r.at[source], at_z(target))

    def w_arrived(distances):
        for distance in distances:
            source = (z + distance) % N
            wz_copy(source, source, 0).wait_recv()
            wc_copy(source, core).start()

    def wc_copy(source, owner):
        return remote(w_block(source, owner), w_block(source, owner), wc_s.at[source], wc_r.at[source], twin)

    for distance, send in first_hop:
        wz_copy(z, (z + distance) % N, send).start()
    wc_copy(z, core).start()

    load_merger.wait()
    for block in range(N):
        value = merger[:, block * PAIR : (block + 1) * PAIR]
        pack_own[block] = value
        pack_swap[block] = pltpu.roll(value.astype(jnp.float32), OWN, 1).astype(jnp.bfloat16)
    swap_inputs = remote(pack_swap, pack_other, core_s.at[0], core_r.at[0], twin)
    swap_inputs.start()

    load_before.wait()

    def activate(block, carry):
        first = pl.multiple_of(block * PAIR, LANES)
        value = gelu(before[:, pl.ds(first, PAIR)].astype(jnp.float32))
        hidden[0, block] = value[:, :PADDED].astype(jnp.bfloat16)
        hidden[1, block] = pltpu.roll(value, OWN, 1)[:, :PADDED].astype(jnp.bfloat16)
        return carry

    lax.fori_loop(0, N, activate, 0)
    swap_hidden = remote(hidden.at[1 - core], other_hidden, core_s.at[1], core_r.at[1], twin)
    swap_hidden.start()

    swap_inputs.wait_recv()
    lane_core = lax.broadcasted_iota(jnp.int32, (SHARE, PAIR), 1) // OWN
    for block in range(N):
        pack_send[block] = jnp.where(
            lane_core == core, pack_own[block].astype(jnp.float32), pack_other[block].astype(jnp.float32)
        ).astype(jnp.bfloat16)

    def pz_copy(target, source):
        return remote(
            pack_send.at[target], inputs.at[source, share, :], pz_s.at[target], pz_r.at[source], at_z(target)
        )

    for step in FAR_FIRST:
        pz_copy((z + step) % N, z).start()
    inputs[z, share, :] = pack_send[z]
    x_send, x_receive, x_finish = ring(
        lambda owner: inputs.at[:, pl.ds(pl.multiple_of(owner * SHARE, SHARE), SHARE), :],
        x, at_x, xu_s, xu_r, xd_s, xd_r,
    )

    limit = before.shape[1] - 2 * LANES
    first = jnp.minimum((roll * UNITS) // LANES * LANES, limit)
    offset = roll * UNITS - first
    window = before[:, pl.ds(pl.multiple_of(first, LANES), 2 * LANES)]
    ids = lax.broadcasted_iota(jnp.int32, (UNITS, 2 * LANES), 1) - lax.broadcasted_iota(
        jnp.int32, (UNITS, 2 * LANES), 0
    )
    select = (ids == offset).astype(jnp.float32).astype(jnp.bfloat16)
    own_before = lax.dot_general(select, window, (((1,), (1,)), ((), ())), preferred_element_type=jnp.float32)
    slope = gelu_slope(own_before)

    w_arrived((2, N - 2))
    for origin, distance, send in second_hop:
        wz_copy((z + origin) % N, (z + distance) % N, send).start()
    w_arrived((1, N - 1))

    def yb_copy(target, source):
        return remote(yb_send.at[target], yb_recv.at[source], yb_s.at[target], yb_r.at[source], at_y(target))

    def xa_copy(target, source):
        return remote(xa_send.at[target], xa_recv.at[source], xa_s.at[target], xa_r.at[source], at_x(target))

    for step in NEAR_FIRST:
        source = (x + step) % N
        xb_copy(source, source).wait_recv()
    xb_recv[x] = xb_send[x]
    for prompt in range(PROMPTS):
        total = xb_recv[PROMPT_X * prompt].astype(jnp.float32) + xb_recv[PROMPT_X * prompt + 1].astype(jnp.float32)
        for part in range(N):
            yb_send[part, prompt] = total[:, part * LANES : (part + 1) * LANES].astype(jnp.bfloat16)

    total = ya_send[y].astype(jnp.float32)
    for step in NEAR_FIRST:
        source = (y + step) % N
        ya_copy(source, source).wait_recv()
        total = total + ya_recv[source].astype(jnp.float32)
    xa_send[...] = total.astype(jnp.bfloat16)
    for step in FAR_FIRST:
        yb_copy((y + step) % N, y).start()
        xa_copy((x + step) % N, x).start()
    xa_recv[x] = xa_send[x]

    for step in NEAR_FIRST:
        source = (z + step) % N
        pz_copy(source, source).wait_recv()
    x_send(0)

    lower = yb_send[y].astype(jnp.float32)
    for step in NEAR_FIRST:
        source = (y + step) % N
        yb_copy(source, source).wait_recv()
        lower = lower + yb_recv[source].astype(jnp.float32)
    for step in NEAR_FIRST:
        source = (x + step) % N
        xa_copy(source, source).wait_recv()
    parts = xa_recv[...].astype(jnp.float32).reshape(PROMPTS, PROMPT_X, ROWS, LANES)
    upper = parts[:, 0] + parts[:, 1]
    merged = jnp.concatenate([upper, lower], axis=1).reshape(MERGED, LANES)
    gathered[y] = merged.astype(jnp.bfloat16)

    def gather_copy(target, source):
        return remote(gathered.at[source], gathered.at[source], gather_s.at[target], gather_r.at[source], at_y(target))

    for step in FAR_FIRST:
        gather_copy((y + step) % N, y).start()
    swap_merged = remote(gathered.at[y], other_merged, core_s.at[2], core_r.at[2], twin)
    swap_merged.start()

    def term_copy(target, source):
        return remote(term_send.at[target], term_recv.at[source], term_s.at[target], term_r.at[source], at_z(target))

    merged_t = merged.T.astype(jnp.bfloat16)
    swap_merged.wait_recv()
    other_t = other_merged[...].astype(jnp.float32).T.astype(jnp.bfloat16)
    swap_hidden.wait_recv()

    rest = PADDED - OWN
    low_lanes = lax.broadcasted_iota(jnp.int32, (LANES // 2, LANES), 1) < LANES - rest

    def second_term(target):
        term = jnp.dot(merged_t, hidden[core, target], preferred_element_type=jnp.float32) + jnp.dot(
            other_t, other_hidden[target], preferred_element_type=jnp.float32
        )
        top = term[: LANES // 2]
        bottom = pltpu.roll(term[LANES // 2 :], rest, 1)
        shared = jnp.where(low_lanes, top[:, PADDED - LANES :], bottom[:, :LANES])
        return jnp.concatenate([top[:, : PADDED - LANES], shared, bottom[:, LANES:]], axis=1)

    for step in FAR_FIRST:
        target = (z + step) % N
        term_send[target] = second_term(target).astype(jnp.bfloat16)
        term_copy(target, z).start()
        if step == FAR_FIRST[HALF]:
            w_arrived((3, N - 3, HALF))
    x_receive(0)
    x_send(1)
    second_total = second_term(z)

    for source in range(N):
        wc_copy(source, 1 - core).wait_recv()
    order = (0,) + NEAR_FIRST
    for pair in range(HALF):
        sources = [(y + step) % N for step in order[2 * pair : 2 * pair + 2]]
        for step, source in zip(order[2 * pair : 2 * pair + 2], sources):
            if step:
                gather_copy(source, source).wait_recv()
        product = lax.dot_general(
            jnp.concatenate([weights[source] for source in sources], axis=1),
            jnp.concatenate([gathered[source] for source in sources], axis=1),
            (((1,), (1,)), ((), ())),
            preferred_element_type=jnp.float32,
        )
        if pair == 0:
            unit_total[...] = product
        elif pair < HALF - 1:
            unit_total[...] += product
        else:
            unit_send[...] = (unit_total[...] + product).astype(jnp.bfloat16).reshape(N, UNITS, MERGED)

    def unit_copy(target, source):
        return remote(
            unit_send.at[target], unit_recv.at[source], unit_s.at[target], unit_r.at[source], at_x(target)
        )

    for step in FAR_FIRST:
        unit_copy((x + step) % N, x).start()
    x_receive(1)
    x_send(2)
    units = unit_send[x].astype(jnp.float32)
    for step in NEAR_FIRST:
        source = (x + step) % N
        unit_copy(source, source).wait_recv()
        units = units + unit_recv[source].astype(jnp.float32)
    grads = (units * slope).astype(jnp.bfloat16)
    pres[core, z] = grads
    pre_ref[...] = grads

    def pre_copy(target, source):
        return remote(
            pres.at[core, source], pres.at[core, source], pre_s.at[target], pre_r.at[source], at_z(target)
        )

    def pt_copy(source, owner):
        return remote(pres.at[owner, source], pres.at[owner, source], pt_s.at[source], pt_r.at[source], twin)

    for step in FAR_FIRST:
        pre_copy((z + step) % N, z).start()
    pt_copy(z, core).start()
    x_receive(2)
    x_send(3)

    for step in NEAR_FIRST:
        source = (z + step) % N
        term_copy(source, source).wait_recv()
        second_total = second_total + term_recv[source].astype(jnp.float32)
    second_total = second_total * factor
    second_ref[:, : LANES // 2] = second_total[:, :PADDED].T[:OWN]
    second_ref[:, LANES // 2 :] = pltpu.roll(second_total[:, PAIR - PADDED :], OWN, 1).T[:OWN]

    for step in NEAR_FIRST:
        source = (z + step) % N
        pre_copy(source, source).wait_recv()
        pt_copy(source, core).start()
    x_receive(3)
    for source in range(N):
        pt_copy(source, 1 - core).wait_recv()
    depth = N * MERGED
    low = jnp.dot(
        jnp.concatenate([pres[0, k] for k in range(N)], axis=1),
        inputs[:, :, :PADDED].reshape(depth, PADDED),
        preferred_element_type=jnp.float32,
    )
    high = jnp.dot(
        jnp.concatenate([pres[1, k] for k in range(N)], axis=1),
        inputs[:, :, PAIR - PADDED :].reshape(depth, PADDED),
        preferred_element_type=jnp.float32,
    )
    first_ref[...] = ((low + pltpu.roll(high, OWN, 1)) * factor)[:, :OWN]

    for step in range(1, N):
        ya_copy((y + step) % N, y).wait_send()
        yb_copy((y + step) % N, y).wait_send()
        xa_copy((x + step) % N, x).wait_send()
        xb_copy((x + step) % N, x).wait_send()
        gather_copy((y + step) % N, y).wait_send()
        unit_copy((x + step) % N, x).wait_send()
        term_copy((z + step) % N, z).wait_send()
        pre_copy((z + step) % N, z).wait_send()
        pz_copy((z + step) % N, z).wait_send()
    for distance, send in first_hop:
        wz_copy(z, (z + distance) % N, send).wait_send()
    for origin, distance, send in second_hop:
        wz_copy((z + origin) % N, (z + distance) % N, send).wait_send()
    x_finish()
    for source in range(N):
        wc_copy(source, core).wait_send()
        pt_copy(source, core).wait_send()

    @pl.when(sender)
    def _():
        for step in range(1, N):
            wy_copy((y + step) % N, y).wait_send()

    for copy in (swap_inputs, swap_hidden, swap_merged):
        copy.wait_send()


def body(row_grads, row_dest, merger_in, hidden_pre, w_second):
    factor = 1.0 / math.sqrt(merger_in.shape[1] * lax.axis_size("enc"))
    width = merger_in.shape[2]
    bf16 = jnp.bfloat16
    vmem = pl.BlockSpec(memory_space=pltpu.VMEM)
    hbm = pl.BlockSpec(memory_space=pltpu.HBM)
    sems = pltpu.SemaphoreType.DMA
    pre, first, second = pl.pallas_call(
        functools.partial(kernel, factor),
        out_shape=(
            jax.ShapeDtypeStruct((UNITS, MERGED), bf16),
            jax.ShapeDtypeStruct((UNITS, OWN), jnp.float32),
            jax.ShapeDtypeStruct((OWN, LANES), jnp.float32),
        ),
        in_specs=[hbm, vmem, hbm, hbm, hbm],
        out_specs=(vmem, vmem, vmem),
        scratch_shapes=[
            pltpu.VMEM((SLOTS, N * N * LANES), bf16),
            pltpu.VMEM((SHARE, width), bf16),
            pltpu.VMEM((MERGED, width), bf16),
            pltpu.VMEM((N, N, ROWS, LANES), bf16),
            pltpu.VMEM((N, N, ROWS, LANES), bf16),
            pltpu.VMEM((N, PROMPTS, ROWS, LANES), bf16),
            pltpu.VMEM((N, PROMPTS, ROWS, LANES), bf16),
            pltpu.VMEM((N, ROWS, LANES), bf16),
            pltpu.VMEM((N, ROWS, LANES), bf16),
            pltpu.VMEM((N, ROWS, N * LANES), bf16),
            pltpu.VMEM((N, ROWS, N * LANES), bf16),
            pltpu.VMEM((N, MERGED, LANES), bf16),
            pltpu.VMEM((MERGED, LANES), bf16),
            pltpu.VMEM((N, PAIR, LANES), bf16),
            pltpu.VMEM((2, N, MERGED, PADDED), bf16),
            pltpu.VMEM((N, MERGED, PADDED), bf16),
            pltpu.VMEM((N, SHARE, PAIR), bf16),
            pltpu.VMEM((N, SHARE, PAIR), bf16),
            pltpu.VMEM((N, SHARE, PAIR), bf16),
            pltpu.VMEM((N, SHARE, PAIR), bf16),
            pltpu.VMEM((N, MERGED, PAIR), bf16),
            pltpu.VMEM((N, LANES // 2, PAIR), bf16),
            pltpu.VMEM((N, LANES // 2, PAIR), bf16),
            pltpu.VMEM((PAIR, MERGED), jnp.float32),
            pltpu.VMEM((N, UNITS, MERGED), bf16),
            pltpu.VMEM((N, UNITS, MERGED), bf16),
            pltpu.VMEM((2, N, UNITS, MERGED), bf16),
            sems((4,)),
        ]
        + [sems((N,)) for _ in range(18)]
        + [sems((HALF,)) for _ in range(4)]
        + [sems((N,)) for _ in range(8)]
        + [sems((3,)), sems((3,))],
        compiler_params=pltpu.CompilerParams(
            collective_id=0, has_side_effects=True, vmem_limit_bytes=54700 * 1024
        ),
    )(row_grads, row_dest, merger_in, hidden_pre, w_second)
    return pre.T[None], first.T, second


def solution(mesh):
    return jax.shard_map(
        body,
        mesh=mesh,
        in_specs=(
            P("enc", "roll", None),
            P("enc", "roll"),
            P("enc", None, None),
            P("enc", None, None),
            P(None, "roll"),
        ),
        out_specs=(P("enc", None, "roll"), P("enc", "roll"), P("enc", "roll")),
        check_vma=False,
    )
```
